32 devices in a mesh: exp: 4 (over z), skyx: 2 (over core), skyy: 4 (over y, x).
Axes of the slice: x: 2, y: 2, z: 4, core: 2. Of those that a mesh axis runs over, the one named last changes fastest.
Arguments:
- estimate: float32 [512, 1024], P('skyx', 'skyy'), may hold values from 0.5 to 102
- observed: float32 [4, 512, 1024], P('exp', 'skyx', 'skyy'), may hold values from 0.25 to 4
- psf_bank: float32 [4, 4, 65, 65], P('exp'), may hold values from 0.1 to 1
- psf_index: int32 [4, 2, 4], P('exp'), may hold values from 0 to 3
- coverage: int32 [4, 2, 4], replicated, may hold values from 0 to 1, as said below
Outputs:
- updated: float32 [512, 1024], P('skyx', 'skyy')
The draws below stay inside these ranges and needn't reach their ends.
Inputs may be any that keep to these rules, and one draw needn't show every extreme that they name: `coverage`: every tile is covered by at least one exposure.
All inputs are finite; a program needn't handle non-finite values.
Results may differ from the reference program's by a relative error of at most 0.0003.
Values sent between devices are 32-bit elements; how exact they have to be, the bound alone decides.
A program may use at most 64 MiB of HBM per device.

```python
import math
import jax
import jax.numpy as jnp
from jax import lax

TILE = 256
RADIUS = 32
PSFS = 4
PSF_SIDE = 65
REGION = 320
SPAN = 384
EXPOSURES = 4
TILES_X = 2
TILES_Y = 4
NX = 512
NY = 1024


def draw_coverage(key, part):
    table_shape = (EXPOSURES, TILES_X, TILES_Y)
    random_bits = jax.random.randint(jax.random.fold_in(key, 11), table_shape, 0, 2)
    leader = jax.random.randint(jax.random.fold_in(key, 12), (TILES_X, TILES_Y), 0, EXPOSURES)
    exposure_rows = lax.broadcasted_iota(jnp.int32, table_shape, 0)
    forced = (exposure_rows == leader[None]).astype(jnp.int32)
    return jnp.maximum(random_bits, forced).astype(jnp.int32)


def draw_estimate(key, part):
    grid_shape = (NX, NY)
    lit_mask = jax.random.randint(jax.random.fold_in(key, 21), grid_shape, 0, 256) == 0
    spread = jax.random.uniform(jax.random.fold_in(key, 22), grid_shape, jnp.float32)
    levels = jax.random.uniform(jax.random.fold_in(key, 23), grid_shape, jnp.float32)
    background = jnp.exp(jnp.log(0.5) + jnp.log(4.0) * spread)
    flux_values = jnp.exp(jnp.log(0.1) + jnp.log(1000.0) * levels)
    return (background + jnp.where(lit_mask, flux_values, 0.0)).astype(jnp.float32)


def plant(entries, stream_key, least, high):
    shape = entries.shape
    place = [jax.random.randint(jax.random.fold_in(stream_key, axis), (), 0, shape[axis]) for axis in range(len(shape))]
    entries = entries.at[tuple(place)].set(least)
    longest = shape.index(max(shape))
    place[longest] = (place[longest] + 1) % shape[longest]
    return entries.at[tuple(place)].set(high)


def level_of(own_key, dims, pieces, least, largest):
    def one(position, blocks):
        heights = jax.random.uniform(jax.random.fold_in(jax.random.fold_in(own_key, 6), position), (blocks,), jnp.float32, least / len(pieces), largest / len(pieces))
        return jnp.repeat(jnp.exp(heights), dims[position] // blocks).reshape((-1,) + (1,) * (len(dims) - position - 1))

    loudness = one(*pieces[0])
    for cut in pieces[1:]:
        loudness = loudness * one(*cut)
    return loudness


def setup_inputs(seed: int = 0) -> dict:
    splits = jax.random.split(jax.random.key(seed), 6)
    return {
        "estimate": draw_estimate(jax.random.fold_in(splits[5], 71), 0),
        "observed": jnp.clip(jnp.exp(math.log(4.0) - 2.7725887 * jax.random.uniform(splits[1], (EXPOSURES, NX, NY), jnp.float32) ** level_of(splits[1], (EXPOSURES, NX, NY), ((0, 4), (1, 2), (2, 4)), -0.2, 0.2)), 0.25, 4.0),
        "psf_bank": jnp.clip(jnp.exp(math.log(1.0) - 2.3025851 * jax.random.uniform(splits[2], (EXPOSURES, PSFS, PSF_SIDE, PSF_SIDE), jnp.float32) ** level_of(splits[2], (EXPOSURES, PSFS, PSF_SIDE, PSF_SIDE), ((0, 4),), -0.2, 0.2)), 0.1, 1.0),
        "psf_index": plant(jax.random.randint(splits[3], (EXPOSURES, TILES_X, TILES_Y), 0, PSFS), jax.random.fold_in(splits[3], 1), 0, PSFS - 1).astype(jnp.int32),
        "coverage": draw_coverage(jax.random.fold_in(splits[5], 71), 0),
    }


def envelope_kernels(psf_bank):
    offsets = jnp.arange(PSF_SIDE, dtype=jnp.float32) - RADIUS
    envelope = jnp.exp(-(offsets[:, None] ** 2 + offsets[None, :] ** 2) / (2.0 * (0.625 * RADIUS) ** 2))
    raw = psf_bank * envelope
    return raw / jnp.sum(raw, axis=(2, 3), keepdims=True)


def to_sky(blocks):
    return blocks.reshape(TILES_X, TILES_Y, TILE, TILE).transpose(0, 2, 1, 3).reshape(NX, NY)


def forward(window, kernel):
    spectrum = jnp.fft.fft2(window, s=(SPAN, SPAN)) * jnp.fft.fft2(kernel, s=(SPAN, SPAN))
    return jnp.real(jnp.fft.ifft2(spectrum))[2 * RADIUS:2 * RADIUS + TILE, 2 * RADIUS:2 * RADIUS + TILE]


def adjoint(window, kernel):
    spectrum = jnp.fft.fft2(window, s=(SPAN, SPAN)) * jnp.conj(jnp.fft.fft2(kernel, s=(SPAN, SPAN)))
    return jnp.real(jnp.fft.ifft2(spectrum))[:TILE, :TILE]


def tile_map(method, padded, tile_kernels):
    flat = tile_kernels.reshape(TILES_X * TILES_Y, PSF_SIDE, PSF_SIDE)

    def single(packed):
        number, kernel = packed
        row_start = (number // TILES_Y) * TILE
        col_start = (number % TILES_Y) * TILE
        window = lax.dynamic_slice(padded, (row_start, col_start), (REGION, REGION))
        return method(window, kernel)

    numbers = jnp.arange(TILES_X * TILES_Y, dtype=jnp.int32)
    return to_sky(lax.map(single, (numbers, flat)))


def reference(estimate, observed, psf_bank, psf_index, coverage):
    kernels_all = envelope_kernels(psf_bank)
    padded = jnp.pad(estimate, RADIUS)

    def per_exposure(total, packed):
        frames, kernels, chosen, cover = packed
        tile_kernels = kernels[chosen]
        blurred = tile_map(forward, padded, tile_kernels)
        mask = jnp.repeat(jnp.repeat(cover.astype(jnp.float32), TILE, 0), TILE, 1)
        ratio = mask * frames / blurred
        back = mask * tile_map(adjoint, jnp.pad(ratio, RADIUS), tile_kernels)
        return total + back, None

    start = jnp.zeros((NX, NY), jnp.float32)
    total = lax.scan(per_exposure, start, (observed, kernels_all, psf_index, coverage))[0]
    covering = jnp.repeat(jnp.repeat(jnp.sum(coverage, 0).astype(jnp.float32), TILE, 0), TILE, 1)
    return estimate * total / covering
```

```python
import functools

import jax
import jax.numpy as jnp
import ml_dtypes
import numpy as np
from jax import lax
from jax.experimental import pallas as pl
from jax.experimental.pallas import tpu as pltpu
from jax.sharding import PartitionSpec as P

MESH = pl.DeviceIdType.MESH
LANES = 128
DIRS = ((0, -1), (0, 1), (-1, 0), (1, 0), (-1, -1), (-1, 1), (1, -1), (1, 1))


def halves(table):
    high = table.astype(ml_dtypes.bfloat16)
    low = (table - high.astype(np.float64)).astype(ml_dtypes.bfloat16)
    return np.stack([high, low])


def make_tables(tile, radius):
    length = tile + 2 * radius
    half = length // 2
    wide = -(-half // LANES) * LANES
    freq = np.arange(half) + 0.5
    center = np.arange(radius, radius + tile)
    places = np.concatenate([center, np.arange(radius), np.arange(radius + tile, length)])
    taps = np.arange(2 * radius + 1) - radius

    def rows(where):
        angle = 2.0 * np.pi / length * np.outer(freq, where)
        return np.concatenate([np.cos(angle), np.sin(angle)])

    def cols(where, depth):
        angle = 2.0 * np.pi / length * np.outer(where, freq)
        table = np.zeros((depth, 2 * wide))
        table[: len(where), :half] = np.cos(angle)
        table[: len(where), wide : wide + half] = np.sin(angle)
        return table

    kern_depth = -(-len(taps) // LANES) * LANES
    kern_rows = np.zeros((length, kern_depth))
    kern_rows[:, : len(taps)] = rows(taps)
    return tuple(
        halves(t)
        for t in (
            cols(places, tile + LANES),
            rows(places),
            cols(center, tile).T.copy(),
            rows(center).T.copy(),
            cols(taps, kern_depth),
            kern_rows,
        )
    )


def split(x):
    high = x.astype(jnp.bfloat16)
    return high, (x - high.astype(jnp.float32)).astype(jnp.bfloat16)


def dot3(a, b):
    def one(x, y):
        return jnp.dot(x, y, preferred_element_type=jnp.float32)

    return one(a[0], b[0]) + (one(a[1], b[0]) + one(a[0], b[1]))


def kernel(
    sizes,
    est_ref, obs_ref, psf_ref, idx_ref, cov_ref,
    h_fc, h_fr, h_ic, h_ir, h_kc, h_kr,
    out_ref,
    t_fc, t_fr, t_ic, t_ir, t_kc, t_kr,
    kpad, kspec, ratio, pack, tb, lr, corner, a_ref, back, slots,
    table_sem, send_sem, recv_sem, rs_send, rs_recv, ag_send, ag_recv,
):
    n_exp, n_x, n_y, radius = sizes
    tile = est_ref.shape[0]
    length = tile + 2 * radius
    half = length // 2
    wide = t_fc.shape[2] // 2
    groups = LANES // radius
    per = tile // groups
    chunk = tile // n_exp
    me = lax.axis_index("exp")
    tx = lax.axis_index("skyx")
    ty = lax.axis_index("skyy")

    def valid(dx, dy):
        x, y = tx + dx, ty + dy
        return (x >= 0) & (x < n_x) & (y >= 0) & (y < n_y)

    def sky(dx, dy):
        return {"skyx": tx + dx, "skyy": ty + dy}

    def peer(d):
        return lax.rem(me + d, n_exp)

    barrier = pltpu.get_barrier_semaphore()
    for dx, dy in DIRS:
        @pl.when(valid(dx, dy))
        def _():
            pl.semaphore_signal(barrier, inc=1, device_id=sky(dx, dy), device_id_type=MESH)
    for d in range(1, n_exp):
        pl.semaphore_signal(barrier, inc=1, device_id={"exp": peer(d)}, device_id_type=MESH)

    loads = [
        pltpu.make_async_copy(source, target, table_sem.at[i])
        for i, (source, target) in enumerate(
            ((h_kc, t_kc), (h_kr, t_kr), (h_fc, t_fc), (h_fr, t_fr), (h_ir, t_ir), (h_ic, t_ic))
        )
    ]
    for load in loads:
        load.start()

    lane = lax.broadcasted_iota(jnp.int32, (per, LANES), 1)
    lane_r = lax.broadcasted_iota(jnp.int32, (radius, LANES), 1)

    def pack_sides(source, turn):
        left = jnp.zeros((per, LANES), jnp.float32)
        right = jnp.zeros((per, LANES), jnp.float32)
        for g in range(groups):
            here = (lane >= g * radius) & (lane < (g + 1) * radius)
            low = source[g * per : (g + 1) * per, 0:LANES]
            high = source[g * per : (g + 1) * per, tile - LANES : tile]
            shift = g * radius
            left = jnp.where(here, pltpu.roll(low, shift, 1) if shift else low, left)
            shift = (g * radius + radius) % LANES
            right = jnp.where(here, pltpu.roll(high, shift, 1) if shift else high, right)
        pack[turn, 0] = left
        pack[turn, 1] = right

    def copies(source, turn):
        ends = (
            (pack.at[turn, 0], lr.at[turn, 1]),
            (pack.at[turn, 1], lr.at[turn, 0]),
            (source.at[0:radius], tb.at[turn, radius : 2 * radius]),
            (source.at[tile - radius : tile], tb.at[turn, 0:radius]),
            (pack.at[turn, 0, 0:radius], corner.at[turn, 3]),
            (pack.at[turn, 1, 0:radius], corner.at[turn, 2]),
            (pack.at[turn, 0, per - radius : per], corner.at[turn, 1]),
            (pack.at[turn, 1, per - radius : per], corner.at[turn, 0]),
        )
        made = []
        for k, ((dx, dy), (src, dst)) in enumerate(zip(DIRS, ends)):
            out = pltpu.make_async_remote_copy(
                src_ref=src, dst_ref=dst, send_sem=send_sem.at[turn, k],
                recv_sem=recv_sem.at[turn, k], device_id=sky(dx, dy), device_id_type=MESH,
            )
            made.append((out, valid(dx, dy), valid(-dx, -dy), dst))
        return made

    def start(made):
        for out, sends, receives, dst in made:
            @pl.when(sends)
            def _():
                out.start()

            @pl.when(jnp.logical_not(receives))
            def _():
                dst[...] = jnp.zeros(dst.shape, jnp.float32)

    def arrive(made):
        for out, sends, receives, dst in made:
            @pl.when(receives)
            def _():
                out.wait_recv()

    def finish(made):
        for out, sends, receives, dst in made:
            @pl.when(sends)
            def _():
                out.wait_send()

    def pair(table, *where):
        return table[(0,) + where], table[(1,) + where]

    every = slice(None)

    def begin(center):
        a_ref[...] = dot3(split(center), pair(t_fc, slice(0, tile), every))

    def sides(turn):
        left, right = lr[turn, 0], lr[turn, 1]
        parts = []
        for g in range(groups):
            shift = (-g * radius) % LANES
            low = pltpu.roll(left, shift, 1) if shift else left
            shift = (radius - g * radius) % LANES
            high = pltpu.roll(right, shift, 1) if shift else right
            parts.append(jnp.where(lane < radius, low, jnp.where(lane < 2 * radius, high, 0.0)))
        return jnp.concatenate(parts, axis=0)

    def corners(turn):
        def row(low, high):
            return jnp.where(
                lane_r < radius, low, jnp.where(lane_r < 2 * radius, high, 0.0)
            )

        top = row(
            pltpu.roll(corner[turn, 0], radius, 1), pltpu.roll(corner[turn, 1], 2 * radius, 1)
        )
        bottom = row(corner[turn, 2], pltpu.roll(corner[turn, 3], radius, 1))
        return jnp.concatenate([top, bottom], axis=0)

    def spectrum(turn):
        outer = pair(t_fc, slice(tile, tile + LANES), every)
        inner = pair(t_fc, slice(0, tile), every)
        mid = split(a_ref[...] + dot3(split(sides(turn)), outer))
        edge = split(dot3(split(tb[turn]), inner) + dot3(split(corners(turn)), outer))
        return dot3(pair(t_fr, every, slice(0, tile)), mid) + dot3(
            pair(t_fr, every, slice(tile, length)), edge
        )

    def combos(z):
        p, q = z[0:half, 0:wide], z[0:half, wide:]
        r, t = z[half:, 0:wide], z[half:, wide:]
        return p - t, r + q, p + t, r - q

    def mix(z, sign):
        u, v, e, d = combos(z)
        ku, kv, ke, kd = kspec[0], kspec[1], kspec[2], kspec[3]
        u2 = u * ku - sign * (v * kv)
        v2 = v * ku + sign * (u * kv)
        e2 = e * ke - sign * (d * kd)
        d2 = d * ke + sign * (e * kd)
        top = jnp.concatenate([u2 + e2, v2 - d2], axis=1)
        bottom = jnp.concatenate([v2 + d2, e2 - u2], axis=1)
        return jnp.concatenate([top, bottom], axis=0)

    def field(z):
        left = dot3(pair(t_ir, every, every), split(z))
        return dot3(split(left), pair(t_ic, every, every))

    pack_sides(est_ref, 0)

    neighbours = n_exp - 1
    for dx, dy in DIRS:
        neighbours = neighbours + valid(dx, dy).astype(jnp.int32)
    pl.semaphore_wait(barrier, neighbours)

    first = copies(est_ref, 0)
    start(first)

    side = psf_ref.shape[-1]
    kpad[...] = jnp.zeros(kpad.shape, jnp.float32)
    kpad[0:side, 0:side] = psf_ref[0, idx_ref[0, tx, ty]]
    at_row = lax.broadcasted_iota(jnp.int32, kpad.shape, 0).astype(jnp.float32) - radius
    at_col = lax.broadcasted_iota(jnp.int32, kpad.shape, 1).astype(jnp.float32) - radius
    envelope = jnp.exp(-(at_row * at_row + at_col * at_col) / (2.0 * (0.625 * radius) ** 2))
    raw = kpad[...] * envelope
    scaled = raw / jnp.sum(raw) * (1.0 / (2.0 * half * half))
    loads[0].wait()
    loads[1].wait()
    k_cols = dot3(split(scaled), pair(t_kc, every, every))
    k_all = dot3(pair(t_kr, every, every), split(k_cols))
    for i, part in enumerate(combos(k_all)):
        kspec[i] = part

    loads[2].wait()
    begin(est_ref[...])
    loads[3].wait()
    loads[4].wait()
    loads[5].wait()

    covering = jnp.float32(0.0)
    for e in range(n_exp):
        covering = covering + cov_ref[e, tx, ty].astype(jnp.float32)
    mine = cov_ref[me, tx, ty].astype(jnp.float32)

    arrive(first)
    blurred = field(mix(spectrum(0), 1.0))
    ratio[...] = mine * obs_ref[0] / blurred
    pack_sides(ratio, 1)
    second = copies(ratio, 1)
    start(second)
    begin(ratio[...])
    arrive(second)
    back[...] = mine * field(mix(spectrum(1), -1.0))

    def block(index):
        return pl.ds(pl.multiple_of(index * chunk, chunk), chunk)

    scatter = []
    for d in range(1, n_exp):
        out = pltpu.make_async_remote_copy(
            src_ref=back.at[block(peer(d))], dst_ref=slots.at[d - 1],
            send_sem=rs_send.at[d - 1], recv_sem=rs_recv.at[d - 1],
            device_id={"exp": peer(d)}, device_id_type=MESH,
        )
        out.start()
        scatter.append(out)
    total = back[block(me), :]
    for d in range(1, n_exp):
        scatter[d - 1].wait_recv()
        total = total + slots[d - 1]
    out_ref[block(me), :] = est_ref[block(me), :] * total / covering
    gather = []
    for d in range(1, n_exp):
        out = pltpu.make_async_remote_copy(
            src_ref=out_ref.at[block(me)], dst_ref=out_ref.at[block(me)],
            send_sem=ag_send.at[d - 1], recv_sem=ag_recv.at[d - 1],
            device_id={"exp": peer(d)}, device_id_type=MESH,
        )
        out.start()
        gather.append(out)
    for d in range(1, n_exp):
        source = peer(n_exp - d)
        pltpu.make_async_remote_copy(
            src_ref=out_ref.at[block(source)], dst_ref=out_ref.at[block(source)],
            send_sem=ag_send.at[d - 1], recv_sem=ag_recv.at[d - 1],
            device_id={"exp": source}, device_id_type=MESH,
        ).wait_recv()
    finish(first)
    finish(second)
    for out in scatter + gather:
        out.wait_send()


def shards(sizes, estimate, observed, psf_bank, psf_index, coverage):
    tile = estimate.shape[0]
    n_exp, n_x, n_y = sizes
    radius = (psf_bank.shape[-1] - 1) // 2
    tables = make_tables(tile, radius)
    length = tile + 2 * radius
    wide = tables[0].shape[2] // 2
    per = tile * radius // LANES
    kern_depth = tables[4].shape[1]
    f32 = jnp.float32
    vmem = pl.BlockSpec(memory_space=pltpu.VMEM)
    smem = pl.BlockSpec(memory_space=pltpu.SMEM)
    hbm = pl.BlockSpec(memory_space=pl.ANY)
    scratch = [pltpu.VMEM(t.shape, jnp.bfloat16) for t in tables] + [
        pltpu.VMEM((kern_depth, kern_depth), f32),
        pltpu.VMEM((4, length // 2, wide), f32),
        pltpu.VMEM((tile, tile), f32),
        pltpu.VMEM((2, 2, per, LANES), f32),
        pltpu.VMEM((2, 2 * radius, tile), f32),
        pltpu.VMEM((2, 2, per, LANES), f32),
        pltpu.VMEM((2, 4, radius, LANES), f32),
        pltpu.VMEM((tile, 2 * wide), f32),
        pltpu.VMEM((tile, tile), f32),
        pltpu.VMEM((max(n_exp - 1, 1), tile // n_exp, tile), f32),
        pltpu.SemaphoreType.DMA((len(tables),)),
        pltpu.SemaphoreType.DMA((2, len(DIRS))),
        pltpu.SemaphoreType.DMA((2, len(DIRS))),
    ] + [pltpu.SemaphoreType.DMA((max(n_exp - 1, 1),))] * 4
    return pl.pallas_call(
        functools.partial(kernel, (n_exp, n_x, n_y, radius)),
        out_shape=jax.ShapeDtypeStruct((tile, tile), f32),
        in_specs=[vmem, vmem, vmem, smem, smem] + [hbm] * len(tables),
        out_specs=vmem,
        scratch_shapes=scratch,
        compiler_params=pltpu.CompilerParams(
            collective_id=0, has_side_effects=True, vmem_limit_bytes=48 * 1024 * 1024
        ),
    )(estimate, observed, psf_bank, psf_index, coverage, *[jnp.asarray(t) for t in tables])


def solution(mesh):
    in_specs = (
        P("skyx", "skyy"),
        P("exp", "skyx", "skyy"),
        P("exp", None, None, None),
        P("exp", None, None),
        P(),
    )
    sizes = tuple(mesh.shape[name] for name in ("exp", "skyx", "skyy"))
    return jax.shard_map(
        functools.partial(shards, sizes),
        mesh=mesh, in_specs=in_specs, out_specs=P("skyx", "skyy"), check_vma=False,
    )
```

```python
import functools

import jax
import jax.numpy as jnp
import ml_dtypes
import numpy as np
from jax import lax
from jax.experimental import pallas as pl
from jax.experimental.pallas import tpu as pltpu
from jax.sharding import PartitionSpec as P

MESH = pl.DeviceIdType.MESH
LANES = 128
DIRS = ((0, -1), (0, 1), (-1, 0), (1, 0), (-1, -1), (-1, 1), (1, -1), (1, 1))


def halves(table):
    high = table.astype(ml_dtypes.bfloat16)
    low = (table - high.astype(np.float64)).astype(ml_dtypes.bfloat16)
    return np.stack([high, low])


def make_tables(tile, radius):
    length = tile + 2 * radius
    half = length // 2
    wide = -(-half // LANES) * LANES
    freq = np.arange(half) + 0.5
    center = np.arange(radius, radius + tile)
    places = np.concatenate([center, np.arange(radius), np.arange(radius + tile, length)])
    taps = np.arange(2 * radius + 1) - radius

    def rows(where):
        angle = 2.0 * np.pi / length * np.outer(freq, where)
        return np.concatenate([np.cos(angle), np.sin(angle)])

    def cols(where, depth):
        angle = 2.0 * np.pi / length * np.outer(where, freq)
        table = np.zeros((depth, 2 * wide))
        table[: len(where), :half] = np.cos(angle)
        table[: len(where), wide : wide + half] = np.sin(angle)
        return table

    kern_depth = -(-len(taps) // LANES) * LANES
    kern_rows = np.zeros((length, kern_depth))
    kern_rows[:, : len(taps)] = rows(taps)
    return tuple(
        halves(t)
        for t in (
            cols(places, tile + LANES),
            rows(places),
            cols(center, tile).T.copy(),
            rows(center).T.copy(),
            cols(taps, kern_depth),
            kern_rows,
        )
    )


def split(x):
    high = x.astype(jnp.bfloat16)
    return high, (x - high.astype(jnp.float32)).astype(jnp.bfloat16)


def dot3(a, b):
    def one(x, y):
        return jnp.dot(x, y, preferred_element_type=jnp.float32)

    return one(a[0], b[0]) + (one(a[1], b[0]) + one(a[0], b[1]))


def kernel(
    sizes,
    h_est, h_obs, h_psf, idx_ref, cov_ref,
    h_fc, h_fr, h_ic, h_ir, h_kc, h_kr,
    out_ref,
    t_fc, t_fr, t_ic, t_ir, t_kc, t_kr, est_ref, obs_ref, psf_ref,
    kpad, kspec, ratio, pack, cpack, tb, lr, corner, a_ref, back, slots,
    table_sem, send_sem, recv_sem, rs_send, rs_recv, ag_send, ag_recv,
):
    n_exp, n_x, n_y, radius = sizes
    tile = est_ref.shape[0]
    length = tile + 2 * radius
    half = length // 2
    wide = t_fc.shape[2] // 2
    groups = LANES // radius
    per = tile // groups
    chunk = tile // n_exp
    me = lax.axis_index("exp")
    tx = lax.axis_index("skyx")
    ty = lax.axis_index("skyy")

    def valid(dx, dy):
        x, y = tx + dx, ty + dy
        return (x >= 0) & (x < n_x) & (y >= 0) & (y < n_y)

    def sky(dx, dy):
        return {"skyx": tx + dx, "skyy": ty + dy}

    def peer(d):
        return lax.rem(me + d, n_exp)

    loads = [
        pltpu.make_async_copy(source, target, table_sem.at[i])
        for i, (source, target) in enumerate(
            (
                (h_est, est_ref), (h_psf, psf_ref), (h_kc, t_kc), (h_kr, t_kr), (h_fc, t_fc),
                (h_fr, t_fr), (h_ir, t_ir), (h_ic, t_ic), (h_obs, obs_ref),
            )
        )
    ]
    for load in loads:
        load.start()

    barrier = pltpu.get_barrier_semaphore()
    for dx, dy in DIRS:
        @pl.when(valid(dx, dy))
        def _():
            pl.semaphore_signal(barrier, inc=1, device_id=sky(dx, dy), device_id_type=MESH)
    for d in range(1, n_exp):
        pl.semaphore_signal(barrier, inc=1, device_id={"exp": peer(d)}, device_id_type=MESH)

    lane = lax.broadcasted_iota(jnp.int32, (per, LANES), 1)
    part = radius // groups
    lane_c = lax.broadcasted_iota(jnp.int32, (part, LANES), 1)

    def pack_sides(source, turn):
        left = jnp.zeros((per, LANES), jnp.float32)
        right = jnp.zeros((per, LANES), jnp.float32)
        for g in range(groups):
            here = (lane >= g * radius) & (lane < (g + 1) * radius)
            low = source[g * per : (g + 1) * per, 0:LANES]
            high = source[g * per : (g + 1) * per, tile - LANES : tile]
            shift = g * radius
            left = jnp.where(here, pltpu.roll(low, shift, 1) if shift else low, left)
            shift = (g * radius + radius) % LANES
            right = jnp.where(here, pltpu.roll(high, shift, 1) if shift else high, right)
        pack[turn, 0] = left
        pack[turn, 1] = right
        for k, block in enumerate(
            (
                left[per - radius : per],
                right[per - radius : per],
                left[0:radius],
                right[0:radius],
            )
        ):
            start_lane = (LANES - radius) if k < 2 else 0
            small = jnp.zeros((part, LANES), jnp.float32)
            for g in range(groups):
                here = (lane_c >= g * radius) & (lane_c < (g + 1) * radius)
                shift = (g * radius - start_lane) % LANES
                piece = block[g * part : (g + 1) * part]
                small = jnp.where(here, pltpu.roll(piece, shift, 1) if shift else piece, small)
            cpack[turn, k] = small

    def copies(source, turn):
        ends = (
            (pack.at[turn, 0], lr.at[turn, 1]),
            (pack.at[turn, 1], lr.at[turn, 0]),
            (source.at[0:radius], tb.at[turn, radius : 2 * radius]),
            (source.at[tile - radius : tile], tb.at[turn, 0:radius]),
            (cpack.at[turn, 2], corner.at[turn, 3]),
            (cpack.at[turn, 3], corner.at[turn, 2]),
            (cpack.at[turn, 0], corner.at[turn, 1]),
            (cpack.at[turn, 1], corner.at[turn, 0]),
        )
        made = []
        for k, ((dx, dy), (src, dst)) in enumerate(zip(DIRS, ends)):
            out = pltpu.make_async_remote_copy(
                src_ref=src, dst_ref=dst, send_sem=send_sem.at[turn, k],
                recv_sem=recv_sem.at[turn, k], device_id=sky(dx, dy), device_id_type=MESH,
            )
            made.append((out, valid(dx, dy), valid(-dx, -dy), dst))
        return made

    def start(made):
        for out, sends, receives, dst in made:
            @pl.when(sends)
            def _():
                out.start()

            @pl.when(jnp.logical_not(receives))
            def _():
                dst[...] = jnp.zeros(dst.shape, jnp.float32)

    def arrive(made):
        for out, sends, receives, dst in made:
            @pl.when(receives)
            def _():
                out.wait_recv()

    def finish(made):
        for out, sends, receives, dst in made:
            @pl.when(sends)
            def _():
                out.wait_send()

    def pair(table, *where):
        return table[(0,) + where], table[(1,) + where]

    every = slice(None)

    def begin(center):
        a_ref[...] = dot3(split(center), pair(t_fc, slice(0, tile), every))

    def sides(turn):
        left, right = lr[turn, 0], lr[turn, 1]
        parts = []
        for g in range(groups):
            shift = (-g * radius) % LANES
            low = pltpu.roll(left, shift, 1) if shift else left
            shift = (radius - g * radius) % LANES
            high = pltpu.roll(right, shift, 1) if shift else right
            parts.append(jnp.where(lane < radius, low, jnp.where(lane < 2 * radius, high, 0.0)))
        return jnp.concatenate(parts, axis=0)

    def corners(turn):
        parts = []
        for low, high in ((corner[turn, 0], corner[turn, 1]), (corner[turn, 2], corner[turn, 3])):
            for g in range(groups):
                shift = (-g * radius) % LANES
                near = pltpu.roll(low, shift, 1) if shift else low
                shift = (radius - g * radius) % LANES
                far = pltpu.roll(high, shift, 1) if shift else high
                parts.append(
                    jnp.where(lane_c < radius, near, jnp.where(lane_c < 2 * radius, far, 0.0))
                )
        return jnp.concatenate(parts, axis=0)

    def spectrum(turn):
        outer = pair(t_fc, slice(tile, tile + LANES), every)
        inner = pair(t_fc, slice(0, tile), every)
        mid = split(a_ref[...] + dot3(split(sides(turn)), outer))
        edge = split(dot3(split(tb[turn]), inner) + dot3(split(corners(turn)), outer))
        return dot3(pair(t_fr, every, slice(0, tile)), mid) + dot3(
            pair(t_fr, every, slice(tile, length)), edge
        )

    def combos(z):
        p, q = z[0:half, 0:wide], z[0:half, wide:]
        r, t = z[half:, 0:wide], z[half:, wide:]
        return p - t, r + q, p + t, r - q

    def mix(z, sign):
        u, v, e, d = combos(z)
        ku, kv, ke, kd = kspec[0], kspec[1], kspec[2], kspec[3]
        u2 = u * ku - sign * (v * kv)
        v2 = v * ku + sign * (u * kv)
        e2 = e * ke - sign * (d * kd)
        d2 = d * ke + sign * (e * kd)
        top = jnp.concatenate([u2 + e2, v2 - d2], axis=1)
        bottom = jnp.concatenate([v2 + d2, e2 - u2], axis=1)
        return jnp.concatenate([top, bottom], axis=0)

    def field(z):
        left = dot3(pair(t_ir, every, every), split(z))
        return dot3(split(left), pair(t_ic, every, every))

    loads[0].wait()
    pack_sides(est_ref, 0)

    neighbours = n_exp - 1
    for dx, dy in DIRS:
        neighbours = neighbours + valid(dx, dy).astype(jnp.int32)
    pl.semaphore_wait(barrier, neighbours)

    first = copies(est_ref, 0)
    start(first)

    side = psf_ref.shape[-1]
    kpad[...] = jnp.zeros(kpad.shape, jnp.float32)
    loads[1].wait()
    model = idx_ref[0, tx, ty]
    chosen = psf_ref[0, :, 0, :]
    for m in range(1, psf_ref.shape[2]):
        chosen = jnp.where(model == m, psf_ref[0, :, m, :], chosen)
    kpad[0:side, 0:side] = chosen
    at_row = lax.broadcasted_iota(jnp.int32, kpad.shape, 0).astype(jnp.float32) - radius
    at_col = lax.broadcasted_iota(jnp.int32, kpad.shape, 1).astype(jnp.float32) - radius
    envelope = jnp.exp(-(at_row * at_row + at_col * at_col) / (2.0 * (0.625 * radius) ** 2))
    raw = kpad[...] * envelope
    scaled = raw / jnp.sum(raw) * (1.0 / (2.0 * half * half))
    loads[2].wait()
    loads[3].wait()
    k_cols = dot3(split(scaled), pair(t_kc, every, every))
    k_all = dot3(pair(t_kr, every, every), split(k_cols))
    for i, term in enumerate(combos(k_all)):
        kspec[i] = term

    loads[4].wait()
    begin(est_ref[...])
    for load in loads[5:]:
        load.wait()

    covering = jnp.float32(0.0)
    for e in range(n_exp):
        covering = covering + cov_ref[e, tx, ty].astype(jnp.float32)
    mine = cov_ref[me, tx, ty].astype(jnp.float32)

    arrive(first)
    blurred = field(mix(spectrum(0), 1.0))
    ratio[...] = mine * obs_ref[0] / blurred
    pack_sides(ratio, 1)
    second = copies(ratio, 1)
    start(second)
    begin(ratio[...])
    arrive(second)
    back[...] = mine * field(mix(spectrum(1), -1.0))

    def block(index):
        return pl.ds(pl.multiple_of(index * chunk, chunk), chunk)

    scatter = []
    for d in range(1, n_exp):
        out = pltpu.make_async_remote_copy(
            src_ref=back.at[block(peer(d))], dst_ref=slots.at[d - 1],
            send_sem=rs_send.at[d - 1], recv_sem=rs_recv.at[d - 1],
            device_id={"exp": peer(d)}, device_id_type=MESH,
        )
        out.start()
        scatter.append(out)
    total = back[block(me), :]
    for d in range(1, n_exp):
        scatter[d - 1].wait_recv()
        total = total + slots[d - 1]
    out_ref[block(me), :] = est_ref[block(me), :] * total / covering
    gather = []
    for d in range(1, n_exp):
        out = pltpu.make_async_remote_copy(
            src_ref=out_ref.at[block(me)], dst_ref=out_ref.at[block(me)],
            send_sem=ag_send.at[d - 1], recv_sem=ag_recv.at[d - 1],
            device_id={"exp": peer(d)}, device_id_type=MESH,
        )
        out.start()
        gather.append(out)
    for d in range(1, n_exp):
        source = peer(n_exp - d)
        pltpu.make_async_remote_copy(
            src_ref=out_ref.at[block(source)], dst_ref=out_ref.at[block(source)],
            send_sem=ag_send.at[d - 1], recv_sem=ag_recv.at[d - 1],
            device_id={"exp": source}, device_id_type=MESH,
        ).wait_recv()
    finish(first)
    finish(second)
    for out in scatter + gather:
        out.wait_send()


def shards(sizes, estimate, observed, psf_bank, psf_index, coverage):
    tile = estimate.shape[0]
    n_exp, n_x, n_y = sizes
    bank = jnp.transpose(psf_bank, (0, 2, 1, 3))
    radius = (psf_bank.shape[-1] - 1) // 2
    tables = make_tables(tile, radius)
    length = tile + 2 * radius
    wide = tables[0].shape[2] // 2
    per = tile * radius // LANES
    kern_depth = tables[4].shape[1]
    f32 = jnp.float32
    vmem = pl.BlockSpec(memory_space=pltpu.VMEM)
    smem = pl.BlockSpec(memory_space=pltpu.SMEM)
    hbm = pl.BlockSpec(memory_space=pltpu.HBM)
    scratch = [pltpu.VMEM(t.shape, jnp.bfloat16) for t in tables] + [
        pltpu.VMEM(estimate.shape, f32),
        pltpu.VMEM(observed.shape, f32),
        pltpu.VMEM(bank.shape, f32),
        pltpu.VMEM((kern_depth, kern_depth), f32),
        pltpu.VMEM((4, length // 2, wide), f32),
        pltpu.VMEM((tile, tile), f32),
        pltpu.VMEM((2, 2, per, LANES), f32),
        pltpu.VMEM((2, 4, radius * radius // LANES, LANES), f32),
        pltpu.VMEM((2, 2 * radius, tile), f32),
        pltpu.VMEM((2, 2, per, LANES), f32),
        pltpu.VMEM((2, 4, radius * radius // LANES, LANES), f32),
        pltpu.VMEM((tile, 2 * wide), f32),
        pltpu.VMEM((tile, tile), f32),
        pltpu.VMEM((max(n_exp - 1, 1), tile // n_exp, tile), f32),
        pltpu.SemaphoreType.DMA((len(tables) + 3,)),
        pltpu.SemaphoreType.DMA((2, len(DIRS))),
        pltpu.SemaphoreType.DMA((2, len(DIRS))),
    ] + [pltpu.SemaphoreType.DMA((max(n_exp - 1, 1),))] * 4
    return pl.pallas_call(
        functools.partial(kernel, (n_exp, n_x, n_y, radius)),
        out_shape=jax.ShapeDtypeStruct((tile, tile), f32),
        in_specs=[hbm, hbm, hbm, smem, smem] + [hbm] * len(tables),
        out_specs=vmem,
        scratch_shapes=scratch,
        compiler_params=pltpu.CompilerParams(
            collective_id=0, has_side_effects=True, vmem_limit_bytes=63 * 1024 * 1024
        ),
    )(estimate, observed, bank, psf_index, coverage, *[jnp.asarray(t) for t in tables])


def solution(mesh):
    in_specs = (
        P("skyx", "skyy"),
        P("exp", "skyx", "skyy"),
        P("exp", None, None, None),
        P("exp", None, None),
        P(),
    )
    sizes = tuple(mesh.shape[name] for name in ("exp", "skyx", "skyy"))
    return jax.shard_map(
        functools.partial(shards, sizes),
        mesh=mesh, in_specs=in_specs, out_specs=P("skyx", "skyy"), check_vma=False,
    )
```

```python
import functools

import jax
import jax.numpy as jnp
import ml_dtypes
import numpy as np
from jax import lax
from jax.experimental import pallas as pl
from jax.experimental.pallas import tpu as pltpu
from jax.sharding import PartitionSpec as P

MESH = pl.DeviceIdType.MESH
LANES = 128
PIECES = 2
DIRS = ((0, -1), (0, 1), (-1, 0), (1, 0), (-1, -1), (-1, 1), (1, -1), (1, 1))


def halves(table):
    high = table.astype(ml_dtypes.bfloat16)
    low = (table - high.astype(np.float64)).astype(ml_dtypes.bfloat16)
    return np.stack([high, low])


def make_tables(tile, radius):
    length = tile + 2 * radius
    half = length // 2
    wide = -(-half // LANES) * LANES
    freq = np.arange(half) + 0.5
    center = np.arange(radius, radius + tile)
    places = np.concatenate([center, np.arange(radius), np.arange(radius + tile, length)])
    taps = np.arange(2 * radius + 1) - radius

    def rows(where):
        angle = 2.0 * np.pi / length * np.outer(freq, where)
        return np.concatenate([np.cos(angle), np.sin(angle)])

    def cols(where, depth):
        angle = 2.0 * np.pi / length * np.outer(where, freq)
        table = np.zeros((depth, 2 * wide))
        table[: len(where), :half] = np.cos(angle)
        table[: len(where), wide : wide + half] = np.sin(angle)
        return table

    kern_depth = -(-len(taps) // LANES) * LANES
    kern_rows = np.zeros((length, kern_depth))
    kern_rows[:, : len(taps)] = rows(taps)
    return tuple(
        halves(t)
        for t in (
            cols(places, tile + LANES),
            rows(places),
            cols(center, tile).T.copy(),
            rows(center).T.copy(),
            cols(taps, kern_depth),
            kern_rows,
        )
    )


def split(x):
    high = x.astype(jnp.bfloat16)
    return high, (x - high.astype(jnp.float32)).astype(jnp.bfloat16)


def dot3(a, b):
    def one(x, y):
        return jnp.dot(x, y, preferred_element_type=jnp.float32)

    return one(a[0], b[0]) + (one(a[1], b[0]) + one(a[0], b[1]))


def kernel(
    sizes,
    h_est, h_obs, h_psf, idx_ref, cov_ref,
    h_fc, h_fr, h_ic, h_ir, h_kc, h_kr,
    out_ref,
    t_fc, t_fr, t_ic, t_ir, t_kc, t_kr, est_ref, obs_ref, psf_ref,
    kpad, kspec, ratio, pack, cpack, tb, lr, corner, a_ref, back, slots,
    table_sem, send_sem, recv_sem, rs_send, rs_recv, ag_send, ag_recv,
):
    n_exp, n_x, n_y, radius = sizes
    tile = est_ref.shape[0]
    length = tile + 2 * radius
    half = length // 2
    wide = t_fc.shape[2] // 2
    groups = LANES // radius
    per = tile // groups
    chunk = tile // n_exp
    me = lax.axis_index("exp")
    tx = lax.axis_index("skyx")
    ty = lax.axis_index("skyy")

    def valid(dx, dy):
        x, y = tx + dx, ty + dy
        return (x >= 0) & (x < n_x) & (y >= 0) & (y < n_y)

    def sky(dx, dy):
        return {"skyx": tx + dx, "skyy": ty + dy}

    def peer(d):
        return lax.rem(me + d, n_exp)

    loads = [
        pltpu.make_async_copy(source, target, table_sem.at[i])
        for i, (source, target) in enumerate(
            (
                (h_est, est_ref), (h_psf, psf_ref), (h_kc, t_kc), (h_kr, t_kr), (h_fc, t_fc),
                (h_fr, t_fr), (h_ir, t_ir), (h_ic, t_ic), (h_obs, obs_ref),
            )
        )
    ]
    for load in loads:
        load.start()

    barrier = pltpu.get_barrier_semaphore()
    for dx, dy in DIRS:
        @pl.when(valid(dx, dy))
        def _():
            pl.semaphore_signal(barrier, inc=1, device_id=sky(dx, dy), device_id_type=MESH)
    for d in range(1, n_exp):
        pl.semaphore_signal(barrier, inc=1, device_id={"exp": peer(d)}, device_id_type=MESH)

    lane = lax.broadcasted_iota(jnp.int32, (per, LANES), 1)
    part = radius // groups
    lane_c = lax.broadcasted_iota(jnp.int32, (part, LANES), 1)

    def pack_sides(source, turn):
        left = jnp.zeros((per, LANES), jnp.float32)
        right = jnp.zeros((per, LANES), jnp.float32)
        for g in range(groups):
            here = (lane >= g * radius) & (lane < (g + 1) * radius)
            low = source[g * per : (g + 1) * per, 0:LANES]
            high = source[g * per : (g + 1) * per, tile - LANES : tile]
            shift = g * radius
            left = jnp.where(here, pltpu.roll(low, shift, 1) if shift else low, left)
            shift = (g * radius + radius) % LANES
            right = jnp.where(here, pltpu.roll(high, shift, 1) if shift else high, right)
        pack[turn, 0] = left
        pack[turn, 1] = right
        for k, block in enumerate(
            (
                left[per - radius : per],
                right[per - radius : per],
                left[0:radius],
                right[0:radius],
            )
        ):
            start_lane = (LANES - radius) if k < 2 else 0
            small = jnp.zeros((part, LANES), jnp.float32)
            for g in range(groups):
                here = (lane_c >= g * radius) & (lane_c < (g + 1) * radius)
                shift = (g * radius - start_lane) % LANES
                piece = block[g * part : (g + 1) * part]
                small = jnp.where(here, pltpu.roll(piece, shift, 1) if shift else piece, small)
            cpack[turn, k] = small

    def copies(source, turn):
        ends = (
            (pack.at[turn, 0], lr.at[turn, 1]),
            (pack.at[turn, 1], lr.at[turn, 0]),
            (source.at[0:radius], tb.at[turn, radius : 2 * radius]),
            (source.at[tile - radius : tile], tb.at[turn, 0:radius]),
            (cpack.at[turn, 2], corner.at[turn, 3]),
            (cpack.at[turn, 3], corner.at[turn, 2]),
            (cpack.at[turn, 0], corner.at[turn, 1]),
            (cpack.at[turn, 1], corner.at[turn, 0]),
        )
        made = []
        for k, ((dx, dy), (src, dst)) in enumerate(zip(DIRS, ends)):
            out = pltpu.make_async_remote_copy(
                src_ref=src, dst_ref=dst, send_sem=send_sem.at[turn, k],
                recv_sem=recv_sem.at[turn, k], device_id=sky(dx, dy), device_id_type=MESH,
            )
            made.append((out, valid(dx, dy), valid(-dx, -dy), dst))
        return made

    def start(made):
        for out, sends, receives, dst in made:
            @pl.when(sends)
            def _():
                out.start()

            @pl.when(jnp.logical_not(receives))
            def _():
                dst[...] = jnp.zeros(dst.shape, jnp.float32)

    def arrive(made):
        for out, sends, receives, dst in made:
            @pl.when(receives)
            def _():
                out.wait_recv()

    def finish(made):
        for out, sends, receives, dst in made:
            @pl.when(sends)
            def _():
                out.wait_send()

    def pair(table, *where):
        return table[(0,) + where], table[(1,) + where]

    every = slice(None)

    def begin(center):
        a_ref[...] = dot3(split(center), pair(t_fc, slice(0, tile), every))

    def sides(turn):
        left, right = lr[turn, 0], lr[turn, 1]
        parts = []
        for g in range(groups):
            shift = (-g * radius) % LANES
            low = pltpu.roll(left, shift, 1) if shift else left
            shift = (radius - g * radius) % LANES
            high = pltpu.roll(right, shift, 1) if shift else right
            parts.append(jnp.where(lane < radius, low, jnp.where(lane < 2 * radius, high, 0.0)))
        return jnp.concatenate(parts, axis=0)

    def corners(turn):
        parts = []
        for low, high in ((corner[turn, 0], corner[turn, 1]), (corner[turn, 2], corner[turn, 3])):
            for g in range(groups):
                shift = (-g * radius) % LANES
                near = pltpu.roll(low, shift, 1) if shift else low
                shift = (radius - g * radius) % LANES
                far = pltpu.roll(high, shift, 1) if shift else high
                parts.append(
                    jnp.where(lane_c < radius, near, jnp.where(lane_c < 2 * radius, far, 0.0))
                )
        return jnp.concatenate(parts, axis=0)

    def spectrum(turn):
        outer = pair(t_fc, slice(tile, tile + LANES), every)
        inner = pair(t_fc, slice(0, tile), every)
        mid = split(a_ref[...] + dot3(split(sides(turn)), outer))
        edge = split(dot3(split(tb[turn]), inner) + dot3(split(corners(turn)), outer))
        return dot3(pair(t_fr, every, slice(0, tile)), mid) + dot3(
            pair(t_fr, every, slice(tile, length)), edge
        )

    def combos(z):
        p, q = z[0:half, 0:wide], z[0:half, wide:]
        r, t = z[half:, 0:wide], z[half:, wide:]
        return p - t, r + q, p + t, r - q

    def mix(z, sign):
        u, v, e, d = combos(z)
        ku, kv, ke, kd = kspec[0], kspec[1], kspec[2], kspec[3]
        u2 = u * ku - sign * (v * kv)
        v2 = v * ku + sign * (u * kv)
        e2 = e * ke - sign * (d * kd)
        d2 = d * ke + sign * (e * kd)
        top = jnp.concatenate([u2 + e2, v2 - d2], axis=1)
        bottom = jnp.concatenate([v2 + d2, e2 - u2], axis=1)
        return jnp.concatenate([top, bottom], axis=0)

    def field(z):
        left = dot3(pair(t_ir, every, every), split(z))
        return dot3(split(left), pair(t_ic, every, every))

    loads[0].wait()
    pack_sides(est_ref, 0)

    neighbours = n_exp - 1
    for dx, dy in DIRS:
        neighbours = neighbours + valid(dx, dy).astype(jnp.int32)
    pl.semaphore_wait(barrier, neighbours)

    first = copies(est_ref, 0)
    start(first)

    side = psf_ref.shape[-1]
    kpad[...] = jnp.zeros(kpad.shape, jnp.float32)
    loads[1].wait()
    model = idx_ref[0, tx, ty]
    chosen = psf_ref[0, :, 0, :]
    for m in range(1, psf_ref.shape[2]):
        chosen = jnp.where(model == m, psf_ref[0, :, m, :], chosen)
    kpad[0:side, 0:side] = chosen
    at_row = lax.broadcasted_iota(jnp.int32, kpad.shape, 0).astype(jnp.float32) - radius
    at_col = lax.broadcasted_iota(jnp.int32, kpad.shape, 1).astype(jnp.float32) - radius
    envelope = jnp.exp(-(at_row * at_row + at_col * at_col) / (2.0 * (0.625 * radius) ** 2))
    raw = kpad[...] * envelope
    scaled = raw / jnp.sum(raw) * (1.0 / (2.0 * half * half))
    loads[2].wait()
    loads[3].wait()
    k_cols = dot3(split(scaled), pair(t_kc, every, every))
    k_all = dot3(pair(t_kr, every, every), split(k_cols))
    for i, term in enumerate(combos(k_all)):
        kspec[i] = term

    loads[4].wait()
    begin(est_ref[...])
    for load in loads[5:]:
        load.wait()

    covering = jnp.float32(0.0)
    for e in range(n_exp):
        covering = covering + cov_ref[e, tx, ty].astype(jnp.float32)
    mine = cov_ref[me, tx, ty].astype(jnp.float32)

    arrive(first)
    blurred = field(mix(spectrum(0), 1.0))
    ratio[...] = mine * obs_ref[0] / blurred
    pack_sides(ratio, 1)
    second = copies(ratio, 1)
    start(second)
    begin(ratio[...])
    arrive(second)
    back[...] = mine * field(mix(spectrum(1), -1.0))

    piece = chunk // PIECES

    def block(index, k):
        return pl.ds(pl.multiple_of(index * chunk + k * piece, piece), piece)

    scatter = {}
    for k in range(PIECES):
        for d in range(1, n_exp):
            at = (d - 1) * PIECES + k
            out = pltpu.make_async_remote_copy(
                src_ref=back.at[block(peer(d), k)], dst_ref=slots.at[at],
                send_sem=rs_send.at[at], recv_sem=rs_recv.at[at],
                device_id={"exp": peer(d)}, device_id_type=MESH,
            )
            out.start()
            scatter[d, k] = out
    gather = []
    for k in range(PIECES):
        here = block(me, k)
        total = back[here, :]
        for d in range(1, n_exp):
            scatter[d, k].wait_recv()
            total = total + slots[(d - 1) * PIECES + k]
        out_ref[here, :] = est_ref[here, :] * total / covering
        for d in range(1, n_exp):
            at = (d - 1) * PIECES + k
            out = pltpu.make_async_remote_copy(
                src_ref=out_ref.at[here], dst_ref=out_ref.at[here],
                send_sem=ag_send.at[at], recv_sem=ag_recv.at[at],
                device_id={"exp": peer(d)}, device_id_type=MESH,
            )
            out.start()
            gather.append(out)
    for k in range(PIECES):
        for d in range(1, n_exp):
            at = (d - 1) * PIECES + k
            source = peer(n_exp - d)
            pltpu.make_async_remote_copy(
                src_ref=out_ref.at[block(source, k)], dst_ref=out_ref.at[block(source, k)],
                send_sem=ag_send.at[at], recv_sem=ag_recv.at[at],
                device_id={"exp": source}, device_id_type=MESH,
            ).wait_recv()
    finish(first)
    finish(second)
    for out in list(scatter.values()) + gather:
        out.wait_send()


def shards(sizes, estimate, observed, psf_bank, psf_index, coverage):
    tile = estimate.shape[0]
    n_exp, n_x, n_y = sizes
    bank = jnp.transpose(psf_bank, (0, 2, 1, 3))
    radius = (psf_bank.shape[-1] - 1) // 2
    tables = make_tables(tile, radius)
    length = tile + 2 * radius
    wide = tables[0].shape[2] // 2
    per = tile * radius // LANES
    kern_depth = tables[4].shape[1]
    f32 = jnp.float32
    vmem = pl.BlockSpec(memory_space=pltpu.VMEM)
    smem = pl.BlockSpec(memory_space=pltpu.SMEM)
    hbm = pl.BlockSpec(memory_space=pltpu.HBM)
    scratch = [pltpu.VMEM(t.shape, jnp.bfloat16) for t in tables] + [
        pltpu.VMEM(estimate.shape, f32),
        pltpu.VMEM(observed.shape, f32),
        pltpu.VMEM(bank.shape, f32),
        pltpu.VMEM((kern_depth, kern_depth), f32),
        pltpu.VMEM((4, length // 2, wide), f32),
        pltpu.VMEM((tile, tile), f32),
        pltpu.VMEM((2, 2, per, LANES), f32),
        pltpu.VMEM((2, 4, radius * radius // LANES, LANES), f32),
        pltpu.VMEM((2, 2 * radius, tile), f32),
        pltpu.VMEM((2, 2, per, LANES), f32),
        pltpu.VMEM((2, 4, radius * radius // LANES, LANES), f32),
        pltpu.VMEM((tile, 2 * wide), f32),
        pltpu.VMEM((tile, tile), f32),
        pltpu.VMEM((max(n_exp - 1, 1) * PIECES, tile // n_exp // PIECES, tile), f32),
        pltpu.SemaphoreType.DMA((len(tables) + 3,)),
        pltpu.SemaphoreType.DMA((2, len(DIRS))),
        pltpu.SemaphoreType.DMA((2, len(DIRS))),
    ] + [pltpu.SemaphoreType.DMA((max(n_exp - 1, 1) * PIECES,))] * 4
    return pl.pallas_call(
        functools.partial(kernel, (n_exp, n_x, n_y, radius)),
        out_shape=jax.ShapeDtypeStruct((tile, tile), f32),
        in_specs=[hbm, hbm, hbm, smem, smem] + [hbm] * len(tables),
        out_specs=vmem,
        scratch_shapes=scratch,
        compiler_params=pltpu.CompilerParams(
            collective_id=0, has_side_effects=True, vmem_limit_bytes=63 * 1024 * 1024
        ),
    )(estimate, observed, bank, psf_index, coverage, *[jnp.asarray(t) for t in tables])


def solution(mesh):
    in_specs = (
        P("skyx", "skyy"),
        P("exp", "skyx", "skyy"),
        P("exp", None, None, None),
        P("exp", None, None),
        P(),
    )
    sizes = tuple(mesh.shape[name] for name in ("exp", "skyx", "skyy"))
    return jax.shard_map(
        functools.partial(shards, sizes),
        mesh=mesh, in_specs=in_specs, out_specs=P("skyx", "skyy"), check_vma=False,
    )
```
